128 devices in a mesh: dp: 16 (over x, y_lo, core), tensor: 8 (over z, y_hi).
Axes of the slice: x: 4, y: 4 (y_hi: 2, y_lo: 2; y = y_hi * 2 + y_lo), z: 4, core: 2. Of those that a mesh axis runs over, the one named last changes fastest.
Arguments:
- hidden_in: bfloat16 [16384, 1024], P('dp'), may hold values from -6 to 6
- out_grad: bfloat16 [16384, 1024], P('dp'), may hold values from -6 to 6
- segments: int32 [16, 1024], P('dp'), may hold values from 0 to 3, never falling along the last dimension, each value on 1 to 512 neighbouring positions
- query_weight: float32 [1024, 1024], P('dp', 'tensor'), may hold values from -0.1875 to 0.1875
- key_projection_weight: float32 [1024, 512], P('dp', 'tensor'), may hold values from -0.1875 to 0.1875
- value_projection_weight: float32 [1024, 512], P('dp', 'tensor'), may hold values from -0.1875 to 0.1875
- out_weight: float32 [1024, 1024], P(('tensor', 'dp')), may hold values from -0.5 to 0.5
- gate_weight: float32 [1024, 4608], P('dp', 'tensor'), may hold values from -0.1875 to 0.1875
- up_weight: float32 [1024, 4608], P('dp', 'tensor'), may hold values from -0.1875 to 0.1875
- down_weight: float32 [4608, 1024], P(('tensor', 'dp')), may hold values from -0.09375 to 0.09375
- norm_gains: float32 [2176], P('dp'), may hold values from 0.5 to 1.5
- query_first: float32 [1024, 1024], P('dp', 'tensor'), may hold values from -16 to 16
- key_moment_first: float32 [1024, 512], P('dp', 'tensor'), may hold values from -16 to 16
- value_moment_first: float32 [1024, 512], P('dp', 'tensor'), may hold values from -48 to 48
- out_first: float32 [1024, 1024], P(('tensor', 'dp')), may hold values from -16 to 16
- gate_first: float32 [1024, 4608], P('dp', 'tensor'), may hold values from -16 to 16
- up_first: float32 [1024, 4608], P('dp', 'tensor'), may hold values from -16 to 16
- down_first: float32 [4608, 1024], P(('tensor', 'dp')), may hold values from -16 to 16
- gains_first: float32 [2176], P('dp'), may hold values from -40 to 40
- query_second: float32 [1024, 1024], P('dp', 'tensor'), may hold values from 34.4064 to 137.6256
- key_moment_second: float32 [1024, 512], P('dp', 'tensor'), may hold values from 34.4064 to 137.6256
- value_moment_second: float32 [1024, 512], P('dp', 'tensor'), may hold values from 278.528 to 1114.112
- out_second: float32 [1024, 1024], P(('tensor', 'dp')), may hold values from 34.4064 to 137.6256
- gate_second: float32 [1024, 4608], P('dp', 'tensor'), may hold values from 34.4064 to 137.6256
- up_second: float32 [1024, 4608], P('dp', 'tensor'), may hold values from 34.4064 to 137.6256
- down_second: float32 [4608, 1024], P(('tensor', 'dp')), may hold values from 34.4064 to 137.6256
- gains_second: float32 [2176], P('dp'), may hold values from 212.992 to 868.352
Outputs:
- block_out: bfloat16 [16384, 1024], P('dp')
- block_input_gradient: float32 [16384, 1024], P(('dp', 'tensor'))
- query_weight_new: float32 [1024, 1024], P('dp', 'tensor')
- query_first_new: float32 [1024, 1024], P('dp', 'tensor')
- query_second_new: float32 [1024, 1024], P('dp', 'tensor')
- key_weight_new: float32 [1024, 512], P('dp', 'tensor')
- key_first_new: float32 [1024, 512], P('dp', 'tensor')
- key_second_new: float32 [1024, 512], P('dp', 'tensor')
- value_weight_new: float32 [1024, 512], P('dp', 'tensor')
- value_first_new: float32 [1024, 512], P('dp', 'tensor')
- value_second_new: float32 [1024, 512], P('dp', 'tensor')
- out_weight_new: float32 [1024, 1024], P(('tensor', 'dp'))
- out_first_new: float32 [1024, 1024], P(('tensor', 'dp'))
- out_second_new: float32 [1024, 1024], P(('tensor', 'dp'))
- gate_weight_new: float32 [1024, 4608], P('dp', 'tensor')
- gate_first_new: float32 [1024, 4608], P('dp', 'tensor')
- gate_second_new: float32 [1024, 4608], P('dp', 'tensor')
- up_weight_new: float32 [1024, 4608], P('dp', 'tensor')
- up_first_new: float32 [1024, 4608], P('dp', 'tensor')
- up_second_new: float32 [1024, 4608], P('dp', 'tensor')
- down_weight_new: float32 [4608, 1024], P(('tensor', 'dp'))
- down_first_new: float32 [4608, 1024], P(('tensor', 'dp'))
- down_second_new: float32 [4608, 1024], P(('tensor', 'dp'))
- gains_new: float32 [2176], P('dp')
- gains_first_new: float32 [2176], P('dp')
- gains_second_new: float32 [2176], P('dp')
The draws below stay inside these ranges and needn't reach their ends.
All inputs are finite; a program needn't handle non-finite values.
Results may differ from the reference program's by a relative error of at most 0.014.
The reference program's roundings to bfloat16 on the way count: a program that leaves them out, or rounds other values in their place, can miss the bound.
Values may be sent and summed in bfloat16 or wider, within the bound.
No kernel may reach another device: no remote copies, remote signals or barrier semaphores. Data moves between devices by JAX's collectives and lax.ppermute only.
A program may use at most 128 MiB of HBM per device.

```python
import math
import jax
import jax.numpy as jnp
import numpy as np
from jax import lax

MODEL_DIMENSION = 1024
QUERY_HEAD_COUNT = 16
KEY_VALUE_HEADS = 8
HEAD_SIZE = 64
FF = 4608
LEN = 1024
DOCS = 4
STEP = 10
SEQUENCES = 16
TOKEN_TOTAL = 16384
GAINS = 2176


def levels(own_key, extent, cuts, low, largest):
    level = 1.0
    for dim, blocks in cuts:
        heights = jax.random.uniform(jax.random.fold_in(jax.random.fold_in(own_key, 6), dim), (blocks,), jnp.float32, low / len(cuts), largest / len(cuts))
        level = level * jnp.repeat(jnp.exp(heights), extent[dim] // blocks).reshape((-1,) + (1,) * (len(extent) - 1 - dim))
    return level


def length_profile(count, total, most, skew):
    weights = [(1 << 20) // math.isqrt(standing ** skew) + 1 for standing in range(2, count + 1)]
    surplus, counts = total - most - (count - 1), [1] * (count - 1)
    while surplus > 0:
        candidates = [i for i in range(count - 1) if counts[i] < most]
        mass, left = sum([weights[i] for i in candidates]), surplus
        for i in candidates:
            addition = min(most - counts[i], max(1, left * weights[i] // mass), surplus)
            counts[i] = counts[i] + addition
            surplus = surplus - addition
    return np.array([most] + counts)


def uneven_parts(rng, amount, total, limit, skew):
    if amount == 2:
        one = jax.random.randint(rng, (), max(1, total - limit), min(limit, total - 1) + 1)
        return jnp.stack([one, total - one])
    tallies = jnp.asarray(length_profile(amount, total, limit, skew), jnp.int32)
    twos = (amount - 1) // 2
    donor, taker = tallies[1:1 + 2 * twos:2], tallies[2:2 + 2 * twos:2]
    margin = jnp.minimum(donor - 1, limit - taker)
    passed = jax.random.randint(jax.random.fold_in(rng, 1), (twos,), 0, 1 << 20) % (margin + 1)
    tallies = tallies.at[1:1 + 2 * twos:2].set(donor - passed).at[2:2 + 2 * twos:2].set(taker + passed)
    return tallies[jax.random.permutation(jax.random.fold_in(rng, 2), amount)]


def normal_values(stream_key, extent, scale, limit, split=(), kind=jnp.bfloat16):
    values = scale * jax.random.normal(stream_key, extent, jnp.float32)
    if split:
        values = values * levels(stream_key, extent, split, -0.22, 0.18)
    return jnp.clip(values, -limit, limit).astype(kind)


def setup_inputs(seed: int = 0) -> dict:
    arg_keys = jax.random.split(jax.random.key(seed), 28)
    return {
        "hidden_in": normal_values(arg_keys[0], (TOKEN_TOTAL, MODEL_DIMENSION), 1.0, 6.0, ((0, 16),)),
        "out_grad": normal_values(arg_keys[1], (TOKEN_TOTAL, MODEL_DIMENSION), 1.0, 6.0, ((0, 16),)),
        "segments": jax.vmap(lambda own: jnp.searchsorted(jnp.cumsum(uneven_parts(own, DOCS, LEN, LEN // 2, 0)), jnp.arange(LEN), side="right"))(jax.random.split(arg_keys[2], SEQUENCES)).reshape((SEQUENCES, LEN)).astype(jnp.int32),
        "query_weight": normal_values(arg_keys[3], (MODEL_DIMENSION, QUERY_HEAD_COUNT * HEAD_SIZE), MODEL_DIMENSION ** -0.5, 0.1875, ((0, 16), (1, 8)), jnp.float32),
        "key_projection_weight": normal_values(arg_keys[4], (MODEL_DIMENSION, KEY_VALUE_HEADS * HEAD_SIZE), MODEL_DIMENSION ** -0.5, 0.1875, ((0, 16), (1, 8)), jnp.float32),
        "value_projection_weight": normal_values(arg_keys[5], (MODEL_DIMENSION, KEY_VALUE_HEADS * HEAD_SIZE), MODEL_DIMENSION ** -0.5, 0.1875, ((0, 16), (1, 8)), jnp.float32),
        "out_weight": normal_values(arg_keys[6], (QUERY_HEAD_COUNT * HEAD_SIZE, MODEL_DIMENSION), (QUERY_HEAD_COUNT * HEAD_SIZE // 8) ** -0.5, 0.5, ((0, 128),), jnp.float32),
        "gate_weight": normal_values(arg_keys[7], (MODEL_DIMENSION, FF), MODEL_DIMENSION ** -0.5, 0.1875, ((0, 16), (1, 8)), jnp.float32),
        "up_weight": normal_values(arg_keys[8], (MODEL_DIMENSION, FF), MODEL_DIMENSION ** -0.5, 0.1875, ((0, 16), (1, 8)), jnp.float32),
        "down_weight": normal_values(arg_keys[9], (FF, MODEL_DIMENSION), FF ** -0.5, 0.09375, ((0, 128),), jnp.float32),
        "norm_gains": jnp.clip(1.0 + 0.1 * jax.random.normal(arg_keys[10], (GAINS,), jnp.float32), 0.5, 1.5),
        "query_first": normal_values(arg_keys[11], (MODEL_DIMENSION, QUERY_HEAD_COUNT * HEAD_SIZE), (0.022 * TOKEN_TOTAL ** 0.5), 16.0, ((0, 16), (1, 8)), jnp.float32),
        "key_moment_first": normal_values(arg_keys[12], (MODEL_DIMENSION, KEY_VALUE_HEADS * HEAD_SIZE), (0.022 * TOKEN_TOTAL ** 0.5), 16.0, ((0, 16), (1, 8)), jnp.float32),
        "value_moment_first": normal_values(arg_keys[13], (MODEL_DIMENSION, KEY_VALUE_HEADS * HEAD_SIZE), (0.062 * TOKEN_TOTAL ** 0.5), 48.0, ((0, 16), (1, 8)), jnp.float32),
        "out_first": normal_values(arg_keys[14], (QUERY_HEAD_COUNT * HEAD_SIZE, MODEL_DIMENSION), (0.022 * TOKEN_TOTAL ** 0.5), 16.0, ((0, 128),), jnp.float32),
        "gate_first": normal_values(arg_keys[15], (MODEL_DIMENSION, FF), (0.022 * TOKEN_TOTAL ** 0.5), 16.0, ((0, 16), (1, 8)), jnp.float32),
        "up_first": normal_values(arg_keys[16], (MODEL_DIMENSION, FF), (0.022 * TOKEN_TOTAL ** 0.5), 16.0, ((0, 16), (1, 8)), jnp.float32),
        "down_first": normal_values(arg_keys[17], (FF, MODEL_DIMENSION), (0.022 * TOKEN_TOTAL ** 0.5), 16.0, ((0, 128),), jnp.float32),
        "gains_first": normal_values(arg_keys[18], (GAINS,), (0.055 * TOKEN_TOTAL ** 0.5), 40.0, ((0, 16),), jnp.float32),
        "query_second": jnp.clip(jnp.exp(math.log(137.6256) - 1.3862944 * jax.random.uniform(arg_keys[19], (MODEL_DIMENSION, QUERY_HEAD_COUNT * HEAD_SIZE), jnp.float32) ** levels(arg_keys[19], (MODEL_DIMENSION, QUERY_HEAD_COUNT * HEAD_SIZE), ((0, 16), (1, 8)), -0.2, 0.2)), 34.4064, 137.6256),
        "key_moment_second": jnp.clip(jnp.exp(math.log(137.6256) - 1.3862944 * jax.random.uniform(arg_keys[20], (MODEL_DIMENSION, KEY_VALUE_HEADS * HEAD_SIZE), jnp.float32) ** levels(arg_keys[20], (MODEL_DIMENSION, KEY_VALUE_HEADS * HEAD_SIZE), ((0, 16), (1, 8)), -0.2, 0.2)), 34.4064, 137.6256),
        "value_moment_second": jnp.clip(jnp.exp(math.log(1114.112) - 1.3862944 * jax.random.uniform(arg_keys[21], (MODEL_DIMENSION, KEY_VALUE_HEADS * HEAD_SIZE), jnp.float32) ** levels(arg_keys[21], (MODEL_DIMENSION, KEY_VALUE_HEADS * HEAD_SIZE), ((0, 16), (1, 8)), -0.2, 0.2)), 278.528, 1114.112),
        "out_second": jnp.clip(jnp.exp(math.log(137.6256) - 1.3862944 * jax.random.uniform(arg_keys[22], (QUERY_HEAD_COUNT * HEAD_SIZE, MODEL_DIMENSION), jnp.float32) ** levels(arg_keys[22], (QUERY_HEAD_COUNT * HEAD_SIZE, MODEL_DIMENSION), ((0, 128),), -0.2, 0.2)), 34.4064, 137.6256),
        "gate_second": jnp.clip(jnp.exp(math.log(137.6256) - 1.3862944 * jax.random.uniform(arg_keys[23], (MODEL_DIMENSION, FF), jnp.float32) ** levels(arg_keys[23], (MODEL_DIMENSION, FF), ((0, 16), (1, 8)), -0.2, 0.2)), 34.4064, 137.6256),
        "up_second": jnp.clip(jnp.exp(math.log(137.6256) - 1.3862944 * jax.random.uniform(arg_keys[24], (MODEL_DIMENSION, FF), jnp.float32) ** levels(arg_keys[24], (MODEL_DIMENSION, FF), ((0, 16), (1, 8)), -0.2, 0.2)), 34.4064, 137.6256),
        "down_second": jnp.clip(jnp.exp(math.log(137.6256) - 1.3862944 * jax.random.uniform(arg_keys[25], (FF, MODEL_DIMENSION), jnp.float32) ** levels(arg_keys[25], (FF, MODEL_DIMENSION), ((0, 128),), -0.2, 0.2)), 34.4064, 137.6256),
        "gains_second": jnp.clip(jnp.exp(math.log(868.352) - 1.40534252 * jax.random.uniform(arg_keys[26], (GAINS,), jnp.float32) ** levels(arg_keys[26], (GAINS,), ((0, 16),), -0.2, 0.2)), 212.992, 868.352),
    }


@jax.custom_vjp
def reduced_dtype(v):
    return lax.optimization_barrier(v.astype(jnp.bfloat16)).astype(jnp.float32)

@jax.custom_vjp
def reduced_backward_dtype(v):
    return v

def low_keep(v):
    return (reduced_dtype(v), None)

def low_pass(kept, grad):
    return (grad,)

def back_keep(v):
    return (v, None)

def back_low(kept, grad):
    return (reduced_dtype(grad),)
reduced_dtype.defvjp(low_keep, low_pass)
reduced_backward_dtype.defvjp(back_keep, back_low)
norm_eps = 1e-05
rope_base = 1000000.0
masked_score = -1e+30
beta_one = 0.9
beta_two = 0.95
adam_eps = 1e-08
matrix_rate = 0.04
gains_rate = 0.4
matrix_decay = 0.1
matmul_precision = lax.Precision.HIGHEST

def rms_apply(vector, gain):
    return vector * lax.rsqrt(lax.optimization_barrier(jnp.mean(vector * vector, axis=-1, keepdims=True)) + norm_eps) * gain

def document_places(segment_ids):
    sequence_length = segment_ids.shape[1]
    places = jnp.broadcast_to(jnp.arange(sequence_length, dtype=jnp.int32)[None, :], segment_ids.shape)
    changed = jnp.concatenate([jnp.ones((segment_ids.shape[0], 1), jnp.int32), (segment_ids[:, 1:] != segment_ids[:, :-1]).astype(jnp.int32)], axis=1)
    starts = lax.cummax(jnp.where(changed > 0, places, 0), axis=1)
    return places - starts

def rotary_tables(place_row, head_dim):
    half_dim = head_dim // 2
    frequency = rope_base ** (-2.0 * jnp.arange(half_dim, dtype=jnp.float32) / head_dim)
    angles = place_row.astype(jnp.float32)[..., None] * frequency
    return (jnp.cos(angles), jnp.sin(angles))

def rotate(vector, cosine, sine):
    half_dim = vector.shape[-1] // 2
    leading = vector[..., :half_dim]
    trailing = vector[..., half_dim:]
    return jnp.concatenate([leading * cosine - trailing * sine, trailing * cosine + leading * sine], axis=-1)

def block_forward(residual_input, seg_row, place_row, params):
    query_w, key_matrix, value_matrix, out_w, gate_w, up_w, down_w, gain_all = [reduced_dtype(member) for member in params]
    sequence_length = residual_input.shape[0]
    model_width = residual_input.shape[1]
    first_norm_gain = gain_all[:model_width]
    second_norm_gain = gain_all[model_width:2 * model_width]
    gain_query = gain_all[2 * model_width:2 * model_width + HEAD_SIZE]
    gain_key = gain_all[2 * model_width + HEAD_SIZE:]
    first_normalized = reduced_dtype(rms_apply(residual_input, first_norm_gain))
    queries = reduced_backward_dtype(jnp.dot(first_normalized, query_w, precision=matmul_precision, preferred_element_type=jnp.float32)).reshape(sequence_length, QUERY_HEAD_COUNT, HEAD_SIZE)
    key_unrotated = reduced_backward_dtype(jnp.dot(first_normalized, key_matrix, precision=matmul_precision, preferred_element_type=jnp.float32)).reshape(sequence_length, KEY_VALUE_HEADS, HEAD_SIZE)
    value_rows = reduced_dtype(reduced_backward_dtype(jnp.dot(first_normalized, value_matrix, precision=matmul_precision, preferred_element_type=jnp.float32))).reshape(sequence_length, KEY_VALUE_HEADS, HEAD_SIZE)
    cosine, sine = rotary_tables(place_row, HEAD_SIZE)
    cosine = cosine[:, None, :]
    sine = sine[:, None, :]
    query_rot = reduced_dtype(rotate(rms_apply(queries, gain_query), cosine, sine))
    key_rot = reduced_dtype(rotate(rms_apply(key_unrotated, gain_key), cosine, sine))
    heads_per_group = QUERY_HEAD_COUNT // KEY_VALUE_HEADS
    key_wide = jnp.repeat(key_rot, heads_per_group, axis=1)
    value_wide = jnp.repeat(value_rows, heads_per_group, axis=1)
    block_rows = min(512, sequence_length)
    places = jnp.arange(sequence_length, dtype=jnp.int32)
    score_scale = HEAD_SIZE ** (-0.5)

    def attend(block_index):
        row_start = block_index * block_rows
        query_block = lax.dynamic_slice_in_dim(query_rot, row_start, block_rows, 0)
        seg_block = lax.dynamic_slice_in_dim(seg_row, row_start, block_rows, 0)
        row_ids = row_start + jnp.arange(block_rows, dtype=jnp.int32)
        scores = reduced_backward_dtype(jnp.einsum('qhd,khd->hqk', query_block, key_wide, precision=matmul_precision) * score_scale)
        allowed = (seg_block[:, None] == seg_row[None, :]) & (places[None, :] <= row_ids[:, None])
        scores = jnp.where(allowed[None], scores, masked_score)
        attn_probs = reduced_dtype(jax.nn.softmax(scores, axis=-1))
        return jnp.einsum('hqk,khd->qhd', attn_probs, value_wide, precision=matmul_precision)
    blocks = lax.map(jax.checkpoint(attend), jnp.arange(sequence_length // block_rows, dtype=jnp.int32))
    mixed = reduced_backward_dtype(reduced_dtype(blocks.reshape(sequence_length, QUERY_HEAD_COUNT * HEAD_SIZE)))
    attn_total = reduced_backward_dtype(jnp.dot(mixed, out_w, precision=matmul_precision, preferred_element_type=jnp.float32))
    residual_middle = residual_input + attn_total
    second_normalized = reduced_dtype(rms_apply(residual_middle, second_norm_gain))
    gate_val = reduced_backward_dtype(jnp.dot(second_normalized, gate_w, precision=matmul_precision, preferred_element_type=jnp.float32))
    up_val = reduced_backward_dtype(jnp.dot(second_normalized, up_w, precision=matmul_precision, preferred_element_type=jnp.float32))
    hidden = reduced_dtype(jax.nn.silu(gate_val) * up_val)
    ffn_total = reduced_backward_dtype(jnp.dot(hidden, down_w, precision=matmul_precision, preferred_element_type=jnp.float32))
    return residual_middle + ffn_total

def adamw(weight, gradient, moment_one, moment_two, step_rate, weight_decay):
    first_new = beta_one * moment_one + (1.0 - beta_one) * gradient
    second_new = beta_two * moment_two + (1.0 - beta_two) * gradient * gradient
    first_fix = 1.0 - beta_one ** STEP
    second_fix = 1.0 - beta_two ** STEP
    update = first_new / first_fix / (jnp.sqrt(second_new / second_fix) + adam_eps) + weight_decay * weight
    return (weight - step_rate * update, first_new, second_new)

def reference(hidden_in, out_grad, segments, query_weight, key_projection_weight, value_projection_weight, out_weight, gate_weight, up_weight, down_weight, norm_gains, query_first, key_moment_first, value_moment_first, out_first, gate_first, up_first, down_first, gains_first, query_second, key_moment_second, value_moment_second, out_second, gate_second, up_second, down_second, gains_second):
    params = (query_weight, key_projection_weight, value_projection_weight, out_weight, gate_weight, up_weight, down_weight, norm_gains)
    inputs = hidden_in.astype(jnp.float32).reshape(SEQUENCES, LEN, MODEL_DIMENSION)
    cotangents = out_grad.astype(jnp.float32).reshape(SEQUENCES, LEN, MODEL_DIMENSION)
    places = document_places(segments)

    def each_sequence(totals, item_set):
        resid_seq, grad_seq, seg_row, place_row = item_set

        def forward_fn(resid_value, param_value):
            return block_forward(resid_value, seg_row, place_row, param_value)
        result, pull_back = jax.vjp(forward_fn, resid_seq, params)
        grad_resid, grad_params = pull_back(grad_seq)
        summed = tuple((left + right for left, right in zip(totals, grad_params)))
        return (summed, (result.astype(jnp.bfloat16), grad_resid))
    zero_grads = tuple((jnp.zeros_like(member) for member in params))
    grads, (results, input_grads) = lax.scan(each_sequence, zero_grads, (inputs, cotangents, segments, places))
    firsts = (query_first, key_moment_first, value_moment_first, out_first, gate_first, up_first, down_first, gains_first)
    seconds = (query_second, key_moment_second, value_moment_second, out_second, gate_second, up_second, down_second, gains_second)
    updated = []
    for position in range(8):
        step_rate = gains_rate if position == 7 else matrix_rate
        weight_decay = 0.0 if position == 7 else matrix_decay
        updated.append(adamw(params[position], grads[position], firsts[position], seconds[position], step_rate, weight_decay))
    return (results.reshape(TOKEN_TOTAL, MODEL_DIMENSION), input_grads.reshape(TOKEN_TOTAL, MODEL_DIMENSION), updated[0][0], updated[0][1], updated[0][2], updated[1][0], updated[1][1], updated[1][2], updated[2][0], updated[2][1], updated[2][2], updated[3][0], updated[3][1], updated[3][2], updated[4][0], updated[4][1], updated[4][2], updated[5][0], updated[5][1], updated[5][2], updated[6][0], updated[6][1], updated[6][2], updated[7][0], updated[7][1], updated[7][2])
```

```python
import functools

import jax
import jax.numpy as jnp
from jax import lax
from jax.experimental import pallas as pl
from jax.experimental.pallas import tpu as pltpu
from jax.sharding import PartitionSpec as P

HEAD_SIZE = 64
STEP = 10

norm_eps = 1e-05
rope_base = 1000000.0
masked_score = -1e30
beta_one = 0.9
beta_two = 0.95
adam_eps = 1e-08
matrix_rate = 0.04
gains_rate = 0.4
matrix_decay = 0.1
score_scale = HEAD_SIZE ** (-0.5)
block = 256
blocks_back = 2
share = 128
gain_rows = 16
f32 = jnp.float32
bf16 = jnp.bfloat16


def dot(left, right):
    return jnp.dot(left, right, preferred_element_type=f32)


def contract_rows(left, right):
    return lax.dot_general(left, right, (((0,), (0,)), ((), ())), preferred_element_type=f32)


def contract_cols(left, right):
    return lax.dot_general(left, right, (((1,), (1,)), ((), ())), preferred_element_type=f32)


def swapped_halves(vector, low):
    return jnp.where(low, pltpu.roll(vector, 96, 1), pltpu.roll(vector, 32, 1))


def head_means(vector, left):
    first = jnp.sum(jnp.where(left, vector, 0.0), axis=1, keepdims=True)
    second = jnp.sum(jnp.where(left, 0.0, vector), axis=1, keepdims=True)
    return jnp.where(left, first, second) * (1.0 / HEAD_SIZE)


def lane_masks(rows):
    lane = lax.broadcasted_iota(jnp.int32, (rows, 128), 1)
    return lane < HEAD_SIZE, lane % HEAD_SIZE < HEAD_SIZE // 2


def allowed_pairs(start, row, first, width):
    keys = lax.broadcasted_iota(jnp.int32, (block, width), 1) + first
    queries = lax.broadcasted_iota(jnp.int32, (block, width), 0) + row
    return (keys <= queries) & (keys >= start)


def attention_kernel(
    x_ref, inv_ref, gain_ref, wq_ref, wkv_ref, turn_ref, start_ref, gqk_ref, wo_ref,
    n1_ref, wide_ref, low_ref, o_ref, sent_ref,
):
    q_ref, k_ref, lse_ref = wide_ref.at[0], wide_ref.at[1], wide_ref.at[2]
    q0_ref, q1_ref, kk_ref, vv_ref = (low_ref.at[i] for i in range(4))
    cos_ref, sin_ref = turn_ref.at[0], turn_ref.at[1]
    gq_ref, gk_ref = gqk_ref.at[pl.ds(0, 1)], gqk_ref.at[pl.ds(1, 1)]
    rows_all = x_ref.shape[0]
    left, low = lane_masks(block)
    for row in range(0, rows_all, block):
        rows = pl.ds(row, block)
        n1 = (x_ref[rows, :].astype(f32) * inv_ref[rows, :] * gain_ref[...]).astype(bf16)
        n1_ref[rows, :] = n1
        q = dot(n1, wq_ref[...])
        kv = dot(n1, wkv_ref[...])
        turned = pltpu.roll(kv, HEAD_SIZE, 1)
        k = jnp.where(left, kv, turned)
        vv_ref[rows, :] = jnp.where(left, turned, kv).astype(bf16)
        q_ref[rows, :] = q
        k_ref[rows, :] = k
        cos, sin = cos_ref[rows, :], sin_ref[rows, :]
        qn = q * lax.rsqrt(head_means(q * q, left) + norm_eps) * gq_ref[...]
        kn = k * lax.rsqrt(jnp.mean(k * k, axis=1, keepdims=True) + norm_eps) * gk_ref[...]
        qr = qn * cos + swapped_halves(qn, low) * sin
        kk_ref[rows, :] = (kn * cos + swapped_halves(kn, low) * sin).astype(bf16)
        q0_ref[rows, :] = jnp.where(left, qr, 0.0).astype(bf16)
        q1_ref[rows, :] = jnp.where(left, 0.0, qr).astype(bf16)
    for row in range(0, rows_all, block):
        rows = pl.ds(row, block)
        first = max(0, row - blocks_back * block)
        width = row + block - first
        keys = pl.ds(first, width)
        kw, vw = kk_ref[keys, :], vv_ref[keys, :]
        allowed = allowed_pairs(start_ref[rows, :], row, first, width)
        outs, sums = [], []
        for qh_ref in (q0_ref, q1_ref):
            sc = contract_cols(qh_ref[rows, :], kw) * score_scale
            sc = jnp.where(allowed, sc, masked_score)
            peak = jnp.max(sc, axis=1, keepdims=True)
            expo = jnp.exp(sc - peak)
            total = jnp.sum(expo, axis=1, keepdims=True)
            outs.append(dot((expo * (1.0 / total)).astype(bf16), vw))
            sums.append(peak + jnp.log(total))
        lse_ref[rows, :] = jnp.where(left, sums[0], sums[1])
        o = jnp.where(left, outs[0], outs[1]).astype(bf16)
        o_ref[rows, :] = o
        sent_ref[rows, :] = dot(o, wo_ref[...]).astype(bf16)


def attention_back_kernel(
    wide_ref, low_ref, dh_ref, turn_ref, start_ref, gqk_ref, wo_ref, o_ref, wq_ref, wkv_ref, x_ref, inv_ref, dg2_ref,
    *refs,
):
    dq_ref, dkv_ref, dwo_ref, sent_ref, dk_sum, dv_sum = refs[-6:]
    q_ref, k_ref, lse_ref = wide_ref.at[0], wide_ref.at[1], wide_ref.at[2]
    q0_ref, q1_ref, kk_ref, vv_ref = (low_ref.at[i] for i in range(4))
    cos_ref, sin_ref = turn_ref.at[0], turn_ref.at[1]
    gq_ref, gk_ref = gqk_ref.at[pl.ds(0, 1)], gqk_ref.at[pl.ds(1, 1)]
    rows_all = q_ref.shape[0]
    left, low = lane_masks(block)
    dk_sum[...] = jnp.zeros_like(dk_sum)
    dv_sum[...] = jnp.zeros_like(dv_sum)
    dwo_ref[...] = jnp.zeros_like(dwo_ref)
    dgq = jnp.zeros((1, 128), f32)
    for row in range(0, rows_all, block):
        rows = pl.ds(row, block)
        first = max(0, row - blocks_back * block)
        width = row + block - first
        keys = pl.ds(first, width)
        kw, vw = kk_ref[keys, :], vv_ref[keys, :]
        allowed = allowed_pairs(start_ref[rows, :], row, first, width)
        dh = dh_ref[rows, :]
        do = contract_cols(dh, wo_ref[...])
        dwo_ref[...] += contract_rows(o_ref[rows, :], dh)
        do_heads = (
            jnp.where(left, do, 0.0).astype(bf16),
            jnp.where(left, 0.0, do).astype(bf16),
        )
        dq_heads = []
        lse = lse_ref[rows, :]
        lse_heads = (lse[:, :1], lse[:, HEAD_SIZE : HEAD_SIZE + 1])
        for qh_ref, lse_h, doh in zip((q0_ref, q1_ref), lse_heads, do_heads):
            qh = qh_ref[rows, :]
            sc = contract_cols(qh, kw) * score_scale
            p = jnp.where(allowed, jnp.exp(jnp.where(allowed, sc, masked_score) - lse_h), 0.0)
            dv_sum[keys, :] += contract_rows(p.astype(bf16), doh)
            dp = contract_cols(doh, vw)
            ds = (p * (dp - jnp.sum(p * dp, axis=1, keepdims=True))).astype(bf16)
            dq_heads.append(dot(ds, kw))
            dk_sum[keys, :] += contract_rows(ds, qh)
        dqr = jnp.where(left, dq_heads[0], dq_heads[1]) * score_scale
        dqn = dqr * cos_ref[rows, :] - swapped_halves(dqr, low) * sin_ref[rows, :]
        q = q_ref[rows, :]
        rq = lax.rsqrt(head_means(q * q, left) + norm_eps)
        qh = q * rq
        dgq = dgq + jnp.sum(dqn * qh, axis=0, keepdims=True)
        scaled = dqn * gq_ref[...]
        dq_ref[rows, :] = (rq * (scaled - qh * head_means(scaled * qh, left))).astype(bf16)
    dgk = jnp.zeros((1, 128), f32)
    dg1 = jnp.zeros((1, x_ref.shape[1]), f32)
    for row in range(0, rows_all, block):
        rows = pl.ds(row, block)
        dkr = dk_sum[rows, :]
        dkr = (dkr + pltpu.roll(dkr, HEAD_SIZE, 1)) * score_scale
        dv = dv_sum[rows, :]
        dv = dv + pltpu.roll(dv, HEAD_SIZE, 1)
        dkn = dkr * cos_ref[rows, :] - swapped_halves(dkr, low) * sin_ref[rows, :]
        k = k_ref[rows, :]
        rk = lax.rsqrt(jnp.mean(k * k, axis=1, keepdims=True) + norm_eps)
        kh = k * rk
        dgk = dgk + jnp.sum(dkn * kh, axis=0, keepdims=True)
        scaled = dkn * gk_ref[...]
        dk = rk * (scaled - kh * jnp.mean(scaled * kh, axis=1, keepdims=True))
        dkv = jnp.where(left, dk, dv).astype(bf16)
        dkv_ref[rows, :] = dkv
        part = contract_cols(dq_ref[rows, :], wq_ref[...]) + contract_cols(dkv, wkv_ref[...])
        part_low = part.astype(bf16)
        for at in range(0, block, share):
            place = (row + at) // share * (share + gain_rows)
            sent_ref[pl.ds(place, share), :] = part_low[at : at + share]
        dg1 = dg1 + jnp.sum(part * (x_ref[rows, :].astype(f32) * inv_ref[rows, :]), axis=0, keepdims=True)
    width = x_ref.shape[1]
    last = jnp.concatenate([dgq, dgk, jnp.zeros((1, width - 256), f32)], axis=1)
    row_id = lax.broadcasted_iota(jnp.int32, (gain_rows, width), 0)
    gains = jnp.where(row_id == 0, dg1, jnp.where(row_id == 1, dg2_ref[...], jnp.where(row_id == 2, last, 0.0)))
    for place in range(share, sent_ref.shape[0], share + gain_rows):
        sent_ref[pl.ds(place, gain_rows), :] = gains.astype(bf16)


def kernel_call(kernel, shapes, scratch, flops, arrays, unread=()):
    whole = [pl.BlockSpec()] * len(arrays)
    return pl.pallas_call(
        kernel,
        out_shape=[jax.ShapeDtypeStruct(s, t) for s, t in shapes],
        in_specs=whole + [pl.BlockSpec(memory_space=pl.ANY)] * len(unread),
        scratch_shapes=scratch,
        compiler_params=pltpu.CompilerParams(vmem_limit_bytes=48 * 1024 * 1024),
        cost_estimate=pl.CostEstimate(flops=flops, bytes_accessed=8 << 20, transcendentals=2 << 20),
    )(*arrays, *unread)


def root_mean_rows(vector):
    inverse = lax.rsqrt(jnp.mean(vector * vector, axis=-1, keepdims=True) + norm_eps)
    return (vector * inverse, inverse)


def root_mean_backward(grad_normed, gain, normed, inverse):
    scaled = grad_normed * gain
    return inverse * (scaled - normed * jnp.mean(scaled * normed, axis=-1, keepdims=True))


def document_starts(segment_row):
    length = segment_row.shape[1]
    places = jnp.arange(length, dtype=jnp.int32)[None, :]
    changed = jnp.concatenate(
        [jnp.ones((1, 1), jnp.bool_), segment_row[:, 1:] != segment_row[:, :-1]], axis=1
    )
    return lax.cummax(jnp.where(changed, places, 0), axis=1)[0]


DP = ("x", "yl", "core")
TENSOR = ("z", "yh")


def sent_to_all(shard, axis):
    copies = jnp.broadcast_to(shard, (lax.axis_size(axis), *shard.shape))
    return lax.all_to_all(copies, axis, split_axis=0, concat_axis=0, tiled=True)


def exchanged(whole, axis):
    devices = lax.axis_size(axis)
    blocks = whole.reshape(devices, whole.shape[0] // devices, *whole.shape[1:])
    return lax.all_to_all(blocks, axis, split_axis=0, concat_axis=0, tiled=True)


def summed(arrived):
    return jnp.sum(arrived.astype(f32), axis=0)


def shifted(value, axis, shift):
    size = lax.axis_size(axis)
    return lax.ppermute(value, axis, [(i, (i + shift) % size) for i in range(size)])


def taken(blocks, index):
    return lax.dynamic_index_in_dim(blocks, index, 0, keepdims=False)


def scattered_by_shifts(blocks, axis):
    size, me = lax.axis_size(axis), lax.axis_index(axis)
    total = taken(blocks, me).astype(f32)
    for shift in range(1, size):
        total = total + shifted(taken(blocks, (me + shift) % size), axis, shift).astype(f32)
    return total


def summed_over_core(part_of):
    core = lax.axis_index("core")
    arrived = shifted(part_of(1 - core), "core", 1)
    return (part_of(core).astype(f32) + arrived.astype(f32)).astype(bf16)


def scattered_over_chips(blocks):
    yl = lax.axis_index("yl")
    over_x = scattered_by_shifts(blocks, "x").astype(bf16)
    return taken(over_x, yl).astype(f32) + shifted(taken(over_x, 1 - yl), "yl", 1).astype(f32)


def adamw(weight, gradient, moment_one, moment_two, step_rate, weight_decay):
    first_new = beta_one * moment_one + (1.0 - beta_one) * gradient
    second_new = beta_two * moment_two + (1.0 - beta_two) * gradient * gradient
    first_fix = 1.0 - beta_one**STEP
    second_fix = 1.0 - beta_two**STEP
    update = (
        first_new / first_fix / (jnp.sqrt(second_new / second_fix) + adam_eps)
        + weight_decay * weight
    )
    return (weight - step_rate * update, first_new, second_new)


def local(
    hidden_in,
    out_grad,
    segments,
    query_weight,
    key_projection_weight,
    value_projection_weight,
    out_weight,
    gate_weight,
    up_weight,
    down_weight,
    norm_gains,
    query_first,
    key_moment_first,
    value_moment_first,
    out_first,
    gate_first,
    up_first,
    down_first,
    gains_first,
    query_second,
    key_moment_second,
    value_moment_second,
    out_second,
    gate_second,
    up_second,
    down_second,
    gains_second,
):
    dp = lax.axis_size(DP)
    ways = lax.axis_size(TENSOR)
    total_rows, width = hidden_in.shape
    units = gate_weight.shape[1]
    share_rows = total_rows // ways
    share_start = lax.axis_index(TENSOR) * share_rows

    def local_portion(whole_rows):
        return lax.dynamic_slice_in_dim(whole_rows, share_start, share_rows, 0)

    owned = norm_gains.shape[0]
    gain_lines = jnp.pad(norm_gains, (0, 2048 - owned)).reshape(16, 128)
    out_lines = out_weight.reshape(8, width // 128, 128).transpose(1, 0, 2).reshape(-1, 128)
    lines = jnp.concatenate(
        [
            query_weight,
            jnp.concatenate([key_projection_weight, value_projection_weight], axis=1),
            gain_lines,
            out_lines,
        ],
        axis=0,
    ).astype(bf16)
    arrived = sent_to_all(lines, DP)
    depth = query_weight.shape[0]
    full_query = arrived[:, :depth].reshape(width, 128)
    full_kv = arrived[:, depth : 2 * depth].reshape(width, 128)
    gains = arrived[:, 2 * depth : 2 * depth + 16].reshape(dp, 2048)[:, :owned].reshape(-1)
    gains = gains.astype(f32)
    out_rows = (
        arrived[:, 2 * depth + 16 :]
        .reshape(dp, width // 128, 8, 128)
        .transpose(0, 2, 1, 3)
        .reshape(-1, width)
    )
    down_rows = down_weight.shape[0]
    half = width // 2
    down_halves = [
        jnp.pad(d, ((0, -down_rows % 8), (0, units - half)))
        for d in (down_weight[:, :half], down_weight[:, half:])
    ]
    ffn_shard = jnp.concatenate([gate_weight, up_weight, *down_halves], axis=0).astype(bf16)
    ffn_whole = lax.all_gather(ffn_shard, DP)
    full_gate = ffn_whole[:, :depth].reshape(width, -1)
    full_up = ffn_whole[:, depth : 2 * depth].reshape(width, -1)
    at, tall_rows = 2 * depth, down_rows + -down_rows % 8
    full_down = jnp.concatenate(
        [ffn_whole[:, p : p + down_rows, :half] for p in (at, at + tall_rows)], axis=2
    ).reshape(-1, width)

    first_gain = gains[:width]
    second_gain = gains[width : 2 * width]
    gain_heads = gains[2 * width :].reshape(2, HEAD_SIZE)
    gain_heads = jnp.concatenate([gain_heads, gain_heads], axis=1)

    x = hidden_in.astype(f32)
    first_inverse = lax.rsqrt(jnp.mean(x * x, axis=-1, keepdims=True) + norm_eps)
    starts = document_starts(segments)
    places = jnp.arange(total_rows, dtype=jnp.int32) - starts
    frequency = rope_base ** (-2.0 * jnp.arange(HEAD_SIZE // 2, dtype=f32) / HEAD_SIZE)
    angles = places.astype(f32)[:, None] * jnp.tile(frequency, 4)[None, :]
    signs = jnp.tile(jnp.repeat(jnp.array([-1.0, 1.0], f32), 32), 2)[None, :]
    turns = jnp.stack([jnp.cos(angles), jnp.sin(angles) * signs])
    starts = starts[:, None]

    tall = (total_rows, 128)
    n1, wide, low, heads, attn_part = kernel_call(
        attention_kernel,
        [((total_rows, width), bf16), ((3, *tall), f32), ((4, *tall), bf16), (tall, bf16), ((total_rows, width), bf16)],
        [],
        1 << 30,
        (hidden_in, first_inverse, first_gain[None, :], full_query, full_kv, turns, starts, gain_heads, out_rows),
    )

    mid_share = local_portion(hidden_in).astype(f32) + summed(exchanged(attn_part, TENSOR))
    second_hat, second_inverse = root_mean_rows(mid_share)
    n2 = sent_to_all((second_hat * second_gain).astype(bf16), TENSOR).reshape(total_rows, width)
    grad_hidden = contract_cols(out_grad, full_down)
    gate = dot(n2, full_gate)
    up = dot(n2, full_up)
    sig = jax.nn.sigmoid(gate)
    silu = gate * sig
    hidden = (silu * up).astype(bf16)
    grad_gate = (grad_hidden * up * sig * (1.0 + gate * (1.0 - sig))).astype(bf16)
    grad_up = (grad_hidden * silu).astype(bf16)
    back_part = (contract_cols(grad_gate, full_gate) + contract_cols(grad_up, full_up)).astype(bf16)
    back_part, grad_gate, grad_up, hidden = lax.optimization_barrier(
        (back_part, grad_gate, grad_up, hidden)
    )
    normed_back = summed(exchanged(back_part, TENSOR))
    mid_grad = local_portion(out_grad).astype(f32) + root_mean_backward(
        normed_back, second_gain, second_hat, second_inverse
    )
    second_gain_part = jnp.sum(normed_back * second_hat, axis=0)
    mid_grad_low = mid_grad.astype(bf16)
    mid_grad_all = sent_to_all(mid_grad_low, TENSOR).reshape(total_rows, width)

    ffn_part = dot(hidden, full_down).astype(bf16)
    over_z = scattered_by_shifts(ffn_part.reshape(4, 2, share_rows, width), "z").astype(bf16)
    yh = lax.axis_index("yh")
    ffn_share = taken(over_z, yh).astype(f32) + shifted(taken(over_z, 1 - yh), "yh", 1).astype(f32)

    gate_part = contract_rows(n2, grad_gate).astype(bf16)
    up_part = contract_rows(n2, grad_up).astype(bf16)
    down_part = contract_rows(hidden, out_grad).astype(bf16)
    gate_part, up_part, down_part, _ = lax.optimization_barrier(
        (gate_part, up_part, down_part, mid_grad_low)
    )

    def for_core(part, core):
        blocks = part.reshape(4, 2, 2, -1, part.shape[1])
        return lax.dynamic_index_in_dim(blocks, core, 2, keepdims=False)

    def gate_up_for(core):
        return jnp.concatenate([for_core(gate_part, core), for_core(up_part, core)], axis=2)

    gate_up_core = summed_over_core(gate_up_for)
    down_core = summed_over_core(functools.partial(for_core, down_part))

    dq, dkv, out_part, sent = kernel_call(
        attention_back_kernel,
        [
            (tall, bf16),
            (tall, bf16),
            ((128, width), f32),
            ((ways * (share + gain_rows), width), bf16),
        ],
        [pltpu.VMEM(tall, f32), pltpu.VMEM(tall, f32)],
        3 << 30,
        (wide, low, mid_grad_all, turns, starts, gain_heads, out_rows, heads)
        + (full_query, full_kv, hidden_in, first_inverse, second_gain_part[None, :]),
    )
    first_arrived = exchanged(sent, TENSOR)
    mid_late, first_arrived = lax.optimization_barrier((mid_share, first_arrived))
    out_share = (mid_late + ffn_share).astype(bf16)
    block_out = sent_to_all(out_share, TENSOR).reshape(total_rows, width)
    first_total = summed(first_arrived)
    first_back = first_total[:share_rows]
    x_share = local_portion(hidden_in).astype(f32)
    inverse_share = local_portion(first_inverse)
    block_input_gradient = mid_grad + root_mean_backward(
        first_back, first_gain, x_share * inverse_share, inverse_share
    )

    gate_up_sum = scattered_over_chips(gate_up_core)
    gate_grad, up_grad = gate_up_sum[:depth], gate_up_sum[depth:]
    down_grad = scattered_over_chips(down_core)

    gains_sums = first_total[share_rows : share_rows + 3]
    gains_part = jnp.concatenate(
        [
            gains_sums[0],
            gains_sums[1],
            gains_sums[2, :HEAD_SIZE] + gains_sums[2, HEAD_SIZE:128],
            gains_sums[2, 128 : 128 + HEAD_SIZE],
        ]
    )
    gains_part = jnp.pad(gains_part.reshape(dp, owned), ((0, 0), (0, 16 * 128 - owned)))
    out_part = out_part.reshape(dp, 8, width // 128, 128).transpose(0, 2, 1, 3)
    last_part = jnp.concatenate(
        [
            contract_rows(n1, dq).reshape(dp, depth, 128),
            contract_rows(n1, dkv).reshape(dp, depth, 128),
            gains_part.reshape(dp, 16, 128),
            out_part.reshape(dp, -1, 128),
        ],
        axis=1,
    ).astype(bf16)
    last = summed(lax.all_to_all(last_part, DP, split_axis=0, concat_axis=0, tiled=True))
    query_grad, kv_grad = last[:depth], last[depth : 2 * depth]
    gains_grad = last[2 * depth : 2 * depth + 16].reshape(-1)[:owned]
    out_grad_w = last[2 * depth + 16 :].reshape(-1, 8, 128).transpose(1, 0, 2).reshape(8, width)

    updated = []
    for weight, gradient, first, second, rate, decay in (
        (query_weight, query_grad, query_first, query_second, matrix_rate, matrix_decay),
        (key_projection_weight, kv_grad[:, :HEAD_SIZE], key_moment_first, key_moment_second, matrix_rate, matrix_decay),
        (value_projection_weight, kv_grad[:, HEAD_SIZE:], value_moment_first, value_moment_second, matrix_rate, matrix_decay),
        (out_weight, out_grad_w, out_first, out_second, matrix_rate, matrix_decay),
        (gate_weight, gate_grad, gate_first, gate_second, matrix_rate, matrix_decay),
        (up_weight, up_grad, up_first, up_second, matrix_rate, matrix_decay),
        (down_weight, down_grad, down_first, down_second, matrix_rate, matrix_decay),
        (norm_gains, gains_grad, gains_first, gains_second, gains_rate, 0.0),
    ):
        updated.extend(adamw(weight, gradient, first, second, rate, decay))
    return (block_out, block_input_gradient, *updated)


def solution(mesh):
    mesh = jax.sharding.Mesh(mesh.devices.reshape(4, 2, 2, 4, 2), (*DP, *TENSOR))
    placed = (
        P(DP, None),
        P(DP, None),
        P(DP, None),
        P(DP, TENSOR),
        P(DP, TENSOR),
        P(DP, TENSOR),
        P((*TENSOR, *DP), None),
        P(DP, TENSOR),
        P(DP, TENSOR),
        P((*TENSOR, *DP), None),
        P(DP),
        P(DP, TENSOR),
        P(DP, TENSOR),
        P(DP, TENSOR),
        P((*TENSOR, *DP), None),
        P(DP, TENSOR),
        P(DP, TENSOR),
        P((*TENSOR, *DP), None),
        P(DP),
        P(DP, TENSOR),
        P(DP, TENSOR),
        P(DP, TENSOR),
        P((*TENSOR, *DP), None),
        P(DP, TENSOR),
        P(DP, TENSOR),
        P((*TENSOR, *DP), None),
        P(DP),
    )
    return jax.shard_map(
        local,
        mesh=mesh,
        in_specs=placed,
        out_specs=(
            P(DP, None),
            P((*DP, *TENSOR), None),
            P(DP, TENSOR),
            P(DP, TENSOR),
            P(DP, TENSOR),
            P(DP, TENSOR),
            P(DP, TENSOR),
            P(DP, TENSOR),
            P(DP, TENSOR),
            P(DP, TENSOR),
            P(DP, TENSOR),
            P((*TENSOR, *DP), None),
            P((*TENSOR, *DP), None),
            P((*TENSOR, *DP), None),
            P(DP, TENSOR),
            P(DP, TENSOR),
            P(DP, TENSOR),
            P(DP, TENSOR),
            P(DP, TENSOR),
            P(DP, TENSOR),
            P((*TENSOR, *DP), None),
            P((*TENSOR, *DP), None),
            P((*TENSOR, *DP), None),
            P(DP),
            P(DP),
            P(DP),
        ),
        check_vma=False,
    )
```
